32 devices in a mesh: row: 4 (over y, core), col: 8 (over z, x).
Axes of the slice: x: 2, y: 2, z: 4, core: 2. Of those that a mesh axis runs over, the one named last changes fastest.
Arguments:
- output_grad: bfloat16 [1024, 8192], P('col', 'row'), may hold values from -16 to 16
- gate_preact: bfloat16 [1024, 28672], P('row', 'col'), may hold values from -6 to 6
- up_preact: bfloat16 [1024, 28672], P('row', 'col'), may hold values from -6 to 6
- gate_weight: bfloat16 [8192, 28672], P('row', 'col'), may hold values from -0.0625 to 0.0625
- up_weight: bfloat16 [8192, 28672], P('row', 'col'), may hold values from -0.0625 to 0.0625
- down_weight: bfloat16 [28672, 8192], P('col', 'row'), may hold values from -0.03125 to 0.03125
Outputs:
- input_grad: bfloat16 [1024, 8192], P('col', 'row')
- gate_factor: float32 [3584, 28672], P('row', 'col')
The draws below stay inside these ranges and needn't reach their ends.
All inputs are finite; a program needn't handle non-finite values.
Results may differ from the reference program's by a relative error of at most 0.0049.
Values may be sent and summed in bfloat16 or wider, within the bound.
A program may use at most 192 MiB of HBM per device.

```python
import jax
import jax.numpy as jnp

D = 8192
FF = 28672
TOKENS = 1024
SLAB = 3584


def block_scale(own_key, extent, pieces, low, high):
    level = 1.0
    for axis_at, shards_of in pieces:
        heights = jax.random.uniform(jax.random.fold_in(jax.random.fold_in(own_key, 6), axis_at), (shards_of,), jnp.float32, low / len(pieces), high / len(pieces))
        level = level * jnp.repeat(jnp.exp(heights), extent[axis_at] // shards_of).reshape((-1,) + (1,) * (len(extent) - 1 - axis_at))
    return level


def noise(key, dims, width, most, split=(), dtype=jnp.bfloat16):
    drawn = width * jax.random.normal(key, dims, jnp.float32)
    if split:
        drawn = drawn * block_scale(key, dims, split, -0.22, 0.18)
    return jnp.clip(drawn, -most, most).astype(dtype)


def setup_inputs(seed: int = 0) -> dict:
    key_list = jax.random.split(jax.random.key(seed), 7)
    return {
        "output_grad": noise(key_list[0], (TOKENS, D), 4.0, 16.0, ((0, 8), (1, 4))),
        "gate_preact": noise(key_list[1], (TOKENS, FF), 1.0, 6.0, ((0, 4), (1, 8))),
        "up_preact": noise(key_list[2], (TOKENS, FF), 1.0, 6.0, ((0, 4), (1, 8))),
        "gate_weight": noise(key_list[3], (D, FF), D ** -0.5, 0.0625, ((0, 4), (1, 8))),
        "up_weight": noise(key_list[4], (D, FF), D ** -0.5, 0.0625, ((0, 4), (1, 8))),
        "down_weight": noise(key_list[5], (FF, D), FF ** -0.5, 0.03125, ((0, 8), (1, 4))),
    }


def swiglu_grads(hidden_grad, gate_preact, up_preact):
    gate_float = gate_preact.astype(jnp.float32)
    up_float = up_preact.astype(jnp.float32)
    logistic = jax.nn.sigmoid(gate_float)
    derivative = logistic * (1.0 + gate_float * (1.0 - logistic))
    grad_gate = (hidden_grad * up_float * derivative).astype(jnp.bfloat16)
    grad_up = (hidden_grad * gate_float * logistic).astype(jnp.bfloat16)
    return grad_gate, grad_up


def reference(output_grad, gate_preact, up_preact, gate_weight, up_weight, down_weight):
    hidden_grad = jnp.dot(output_grad, down_weight.T, preferred_element_type=jnp.float32)
    grad_gate, grad_up = swiglu_grads(hidden_grad, gate_preact, up_preact)
    input_float = jnp.dot(grad_gate, gate_weight.T, preferred_element_type=jnp.float32)
    input_float = input_float + jnp.dot(grad_up, up_weight.T, preferred_element_type=jnp.float32)
    input_grad = input_float.astype(jnp.bfloat16)
    slab_grads = grad_gate[:, 0:SLAB]
    gate_factor = jnp.dot(slab_grads.T, grad_gate, preferred_element_type=jnp.float32) / TOKENS
    return input_grad, gate_factor
```

```python
import jax
import jax.numpy as jnp
from jax import lax
from jax.sharding import PartitionSpec as P

CHUNKS = 2


def contract_last(left, right):
    return lax.dot_general(
        left, right, (((1,), (1,)), ((), ())), preferred_element_type=jnp.float32
    )


def swap(block, axis, size, bit):
    return lax.ppermute(block, axis, [(i, i ^ bit) for i in range(size)])


def halves(blocks, bit_value):
    pairs = blocks.reshape((blocks.shape[0] // 2, 2) + blocks.shape[1:])
    other = lax.dynamic_index_in_dim(pairs, 1 - bit_value, 1, keepdims=False)
    own = lax.dynamic_index_in_dim(pairs, bit_value, 1, keepdims=False)
    return other, own


def flat(blocks):
    return blocks.reshape((-1, blocks.shape[-1]))


def halving(product, operands, axis, size):
    index = lax.axis_index(axis)
    m = operands[0].shape[1]
    received = []
    bit = 1
    while bit < size:
        bit_value = (index // bit) % 2
        split = [halves(x, bit_value) for x in operands]
        split_received = [halves(x, bit_value) for x in received]
        sent = product(*[flat(other) for other, _ in split])
        for other, _ in split_received:
            sent = sent + flat(other).astype(jnp.float32)
        sent = swap(sent.astype(jnp.bfloat16), axis, size, bit)
        operands = [own for _, own in split]
        received = [own for _, own in split_received]
        received.append(sent.reshape((-1, m, sent.shape[-1])))
        bit *= 2
    total = product(*[flat(x) for x in operands])
    for x in received:
        total = total + flat(x).astype(jnp.float32)
    return total


def doubling(block, axis, size):
    index = lax.axis_index(axis)
    blocks = block[None]
    bit = size // 2
    while bit:
        other = swap(blocks, axis, size, bit)
        low = (index // bit) % 2 == 0
        first = jnp.where(low, blocks, other)
        second = jnp.where(low, other, blocks)
        blocks = jnp.stack([first, second], axis=1).reshape((-1,) + block.shape)
        bit //= 2
    return blocks


def swiglu_grads(hidden_grad, gate_preact, up_preact):
    gate_float = gate_preact.astype(jnp.float32)
    up_float = up_preact.astype(jnp.float32)
    logistic = jax.nn.sigmoid(gate_float)
    derivative = logistic * (1.0 + gate_float * (1.0 - logistic))
    grad_gate = (hidden_grad * up_float * derivative).astype(jnp.bfloat16)
    grad_up = (hidden_grad * gate_float * logistic).astype(jnp.bfloat16)
    return (grad_gate, grad_up)


def from_root(block, axis, holder):
    block = jnp.where(lax.axis_index(axis) == holder, block, jnp.zeros_like(block))
    return lax.psum(block, axis)


def make_shards(rows, cols, tokens, slab_dev):
    def shards(output_grad, gate_preact, up_preact, gate_weight, up_weight, down_weight):
        units_dev = gate_weight.shape[1]
        part = output_grad.shape[0] // CHUNKS
        cols_per_row = cols // rows
        first_unit = lax.axis_index("row") * slab_dev
        owner_column = first_unit // units_dev
        offset = first_unit % units_dev

        def local_tokens(preact, h):
            split = preact.reshape((cols_per_row, CHUNKS, part, preact.shape[1]))
            return split[:, h].reshape((cols_per_row * part, preact.shape[1]))

        cotangents = [
            lax.all_gather(output_grad[h * part : (h + 1) * part], "col", axis=0, tiled=True)
            for h in range(CHUNKS)
        ]
        slabs, gates, outs = [], [], []
        for h in range(CHUNKS):
            cotangent = cotangents[h].reshape((rows, -1, output_grad.shape[1]))
            hidden_grad = halving(
                lambda x: contract_last(x, down_weight), [cotangent], "row", rows
            )
            grad_gate, grad_up = swiglu_grads(
                hidden_grad, local_tokens(gate_preact, h), local_tokens(up_preact, h)
            )
            gate_all = flat(doubling(grad_gate, "row", rows))
            own_slab = lax.dynamic_slice_in_dim(gate_all, offset, slab_dev, 1)
            slabs.append(from_root(own_slab, "col", owner_column))
            gates.append(gate_all)
            up_all = flat(doubling(grad_up, "row", rows))
            outs.append(
                halving(
                    lambda g, u: contract_last(g, gate_weight) + contract_last(u, up_weight),
                    [gate_all.reshape((cols, part, -1)), up_all.reshape((cols, part, -1))],
                    "col",
                    cols,
                )
            )
        factor = 0.0
        for slab, gate in zip(slabs, gates):
            factor = factor + lax.dot_general(
                slab, gate, (((0,), (0,)), ((), ())), preferred_element_type=jnp.float32
            )
        input_grad = jnp.concatenate([x.astype(jnp.bfloat16) for x in outs], axis=0)
        return (input_grad, factor / tokens)

    return shards


def solution(mesh):
    rows, cols = mesh.shape["row"], mesh.shape["col"]

    def run(output_grad, gate_preact, up_preact, gate_weight, up_weight, down_weight):
        tokens = output_grad.shape[0]
        shards = make_shards(rows, cols, tokens, SLAB_DEV)
        return jax.shard_map(
            shards,
            mesh=mesh,
            in_specs=(
                P("col", "row"),
                P("row", "col"),
                P("row", "col"),
                P("row", "col"),
                P("row", "col"),
                P("col", "row"),
            ),
            out_specs=(P("col", "row"), P("row", "col")),
            check_vma=False,
        )(output_grad, gate_preact, up_preact, gate_weight, up_weight, down_weight)

    return run


SLAB_DEV = 896
```

```python
import jax
import jax.numpy as jnp
from jax import lax
from jax.sharding import PartitionSpec as P

CHUNKS = 2
SLAB_DEV = 896


def contract_last(left, right):
    return lax.dot_general(
        left, right, (((1,), (1,)), ((), ())), preferred_element_type=jnp.float32
    )


def swap(block, axis, size, bit):
    return lax.ppermute(block, axis, [(i, i ^ bit) for i in range(size)])


def bits_down(size):
    bit = size // 2
    while bit:
        yield bit
        bit //= 2


def gather_relative(block, axis, size):
    pieces = {0: block}
    for bit in bits_down(size):
        for k in sorted(pieces):
            pieces[k | bit] = swap(pieces[k], axis, size, bit)
    return [pieces[k] for k in range(size)]


def halving_order(size):
    if size == 1:
        return [0]
    rest = halving_order(size // 2)
    return [2 * k + 1 for k in rest] + [2 * k for k in rest]


def halving(total, axis, size):
    m = total.shape[0] // size
    received = []
    bit, left = 1, size
    while left > 1:
        half = left // 2 * m
        sent = total[:half]
        for x in received:
            sent = sent + x[:half].astype(jnp.float32)
        received = [x[half:] for x in received]
        received.append(swap(sent.astype(jnp.bfloat16), axis, size, bit))
        total = total[half:]
        bit, left = bit * 2, left // 2
    for x in received:
        total = total + x.astype(jnp.float32)
    return total


def pick(stacked, index, m):
    return lax.dynamic_slice_in_dim(stacked, index * m, m, 0)


def swiglu_grads(hidden_grad, gate_preact, up_preact):
    gate_float = gate_preact.astype(jnp.float32)
    up_float = up_preact.astype(jnp.float32)
    logistic = jax.nn.sigmoid(gate_float)
    derivative = logistic * (1.0 + gate_float * (1.0 - logistic))
    grad_gate = (hidden_grad * up_float * derivative).astype(jnp.bfloat16)
    grad_up = (hidden_grad * gate_float * logistic).astype(jnp.bfloat16)
    return (grad_gate, grad_up)


def make_shards(rows, cols):
    def shards(output_grad, gate_preact, up_preact, gate_weight, up_weight, down_weight):
        units_dev = gate_weight.shape[1]
        part = output_grad.shape[0] // CHUNKS
        tokens = output_grad.shape[0] * cols
        per_row = cols // rows
        row, col = lax.axis_index("row"), lax.axis_index("col")
        offset = (row * SLAB_DEV) % units_dev
        holders = [r * SLAB_DEV // units_dev for r in range(rows)]
        from_holder = col ^ ((row * SLAB_DEV) // units_dev)

        def broadcast(slab):
            for bit in bits_down(cols):
                pairs = [
                    (r * cols + (holders[r] ^ k), r * cols + (holders[r] ^ k ^ bit))
                    for r in range(rows)
                    for k in range(0, cols, 2 * bit)
                ]
                arrived = lax.ppermute(slab, ("row", "col"), pairs)
                slab = jnp.where(from_holder % (2 * bit) == bit, arrived, slab)
            return slab

        def local_tokens(preact, h):
            split = preact.reshape((per_row, CHUNKS, part, preact.shape[1]))
            return split[:, h].reshape((per_row * part, preact.shape[1]))

        def cotangent(h):
            pieces = gather_relative(output_grad[h * part : (h + 1) * part], "col", cols)
            stacked = jnp.concatenate(pieces, axis=0)
            wanted = [
                col ^ ((row ^ j) * per_row + sub)
                for j in halving_order(rows)
                for sub in range(per_row)
            ]
            return jnp.concatenate([pick(stacked, k, part) for k in wanted], axis=0)

        def scatter(total):
            blocks = []
            for k in halving_order(cols):
                target = col ^ k
                position = (row ^ (target // per_row)) * per_row + target % per_row
                blocks.append(pick(total, position, part))
            return halving(jnp.concatenate(blocks, axis=0), "col", cols)

        hidden = [
            halving(contract_last(cotangent(h), down_weight), "row", rows) for h in range(CHUNKS)
        ]
        grads = [
            swiglu_grads(hidden[h], local_tokens(gate_preact, h), local_tokens(up_preact, h))
            for h in range(CHUNKS)
        ]
        gates, slabs, outs = [], [], []
        for h in range(CHUNKS):
            gates.append(jnp.concatenate(gather_relative(grads[h][0], "row", rows), axis=0))
            slabs.append(broadcast(lax.dynamic_slice_in_dim(gates[h], offset, SLAB_DEV, 1)))
        for h in range(CHUNKS):
            up_all = jnp.concatenate(gather_relative(grads[h][1], "row", rows), axis=0)
            outs.append(
                scatter(contract_last(gates[h], gate_weight) + contract_last(up_all, up_weight))
            )
        factor = lax.dot_general(
            jnp.concatenate(slabs, axis=0),
            jnp.concatenate(gates, axis=0),
            (((0,), (0,)), ((), ())),
            preferred_element_type=jnp.float32,
        )
        input_grad = jnp.concatenate([x.astype(jnp.bfloat16) for x in outs], axis=0)
        return (input_grad, factor / tokens)

    return shards


def solution(mesh):
    return jax.shard_map(
        make_shards(mesh.shape["row"], mesh.shape["col"]),
        mesh=mesh,
        in_specs=(
            P("col", "row"),
            P("row", "col"),
            P("row", "col"),
            P("row", "col"),
            P("row", "col"),
            P("col", "row"),
        ),
        out_specs=(P("col", "row"), P("row", "col")),
        check_vma=False,
    )
```

```python
import jax
import jax.numpy as jnp
from jax import lax
from jax.sharding import PartitionSpec as P

CHUNKS = 2
SLAB_DEV = 896


def contract_last(left, right):
    return lax.dot_general(
        left, right, (((1,), (1,)), ((), ())), preferred_element_type=jnp.float32
    )


def swap(block, axis, size, bit):
    return lax.ppermute(block, axis, [(i, i ^ bit) for i in range(size)])


def bits_down(size):
    bit = size // 2
    while bit:
        yield bit
        bit //= 2


def gather_relative(block, axis, size):
    pieces = {0: block}
    for bit in bits_down(size):
        for k in sorted(pieces):
            pieces[k | bit] = swap(pieces[k], axis, size, bit)
    return [pieces[k] for k in range(size)]


def halving_order(size):
    if size == 1:
        return [0]
    rest = halving_order(size // 2)
    return [2 * k + 1 for k in rest] + [2 * k for k in rest]


def after(value, *earlier):
    return lax.optimization_barrier((value,) + earlier)[0]


def halving(total, axis, size):
    m = total.shape[0] // size
    last = None
    received = []
    bit, left = 1, size
    while left > 1:
        half = left // 2 * m
        sent = total[:half]
        for x in received:
            sent = sent + x[:half].astype(jnp.float32)
        received = [x[half:] for x in received]
        last = sent.astype(jnp.bfloat16)
        received.append(swap(last, axis, size, bit))
        total = total[half:]
        bit, left = bit * 2, left // 2
    for x in received:
        total = total + x.astype(jnp.float32)
    return total, last


def pick(stacked, index, m):
    return lax.dynamic_slice_in_dim(stacked, index * m, m, 0)


def swiglu_grads(hidden_grad, gate_preact, up_preact):
    gate_float = gate_preact.astype(jnp.float32)
    up_float = up_preact.astype(jnp.float32)
    logistic = jax.nn.sigmoid(gate_float)
    derivative = logistic * (1.0 + gate_float * (1.0 - logistic))
    grad_gate = (hidden_grad * up_float * derivative).astype(jnp.bfloat16)
    grad_up = (hidden_grad * gate_float * logistic).astype(jnp.bfloat16)
    return (grad_gate, grad_up)


def make_shards(rows, cols):
    def shards(output_grad, gate_preact, up_preact, gate_weight, up_weight, down_weight):
        units_dev = gate_weight.shape[1]
        part = output_grad.shape[0] // CHUNKS
        tokens = output_grad.shape[0] * cols
        per_row = cols // rows
        row, col = lax.axis_index("row"), lax.axis_index("col")
        offset = (row * SLAB_DEV) % units_dev
        holders = [r * SLAB_DEV // units_dev for r in range(rows)]
        from_holder = col ^ ((row * SLAB_DEV) // units_dev)

        def broadcast(slab):
            steps, unseen = [], cols - 1
            for bit in [1] + [b for b in bits_down(cols) if b > 1]:
                reached = [k for k in range(cols) if not k & unseen]
                pairs = [
                    (r * cols + (holders[r] ^ k), r * cols + (holders[r] ^ k ^ bit))
                    for r in range(rows)
                    for k in reached
                ]
                unseen -= bit
                arrived = lax.ppermute(slab, ("row", "col"), pairs)
                here = ((from_holder & bit) != 0) & ((from_holder & unseen) == 0)
                slab = jnp.where(here, arrived, slab)
                steps.append(slab)
            return steps

        def local_tokens(preact, h):
            split = preact.reshape((per_row, CHUNKS, part, preact.shape[1]))
            return split[:, h].reshape((per_row * part, preact.shape[1]))

        def cotangent(h):
            pieces = gather_relative(output_grad[h * part : (h + 1) * part], "col", cols)
            stacked = jnp.concatenate(pieces, axis=0)
            wanted = [
                col ^ ((row ^ j) * per_row + sub)
                for j in halving_order(rows)
                for sub in range(per_row)
            ]
            return jnp.concatenate([pick(stacked, k, part) for k in wanted], axis=0)

        def scatter(total):
            blocks = []
            for k in halving_order(cols):
                target = col ^ k
                position = (row ^ (target // per_row)) * per_row + target % per_row
                blocks.append(pick(total, position, part))
            return halving(jnp.concatenate(blocks, axis=0), "col", cols)[0]

        def gather(block):
            return jnp.concatenate(gather_relative(block, "row", rows), axis=0)

        grads, earlier = [], ()
        for h in range(CHUNKS):
            part_sum = contract_last(after(cotangent(h), *earlier), down_weight)
            hidden_grad, last = halving(part_sum, "row", rows)
            earlier = (last,)
            grads.append(
                swiglu_grads(hidden_grad, local_tokens(gate_preact, h), local_tokens(up_preact, h))
            )
        gates = [gather(grad_gate) for grad_gate, _ in grads]
        slabs = [
            broadcast(lax.dynamic_slice_in_dim(gate, offset, SLAB_DEV, 1)) for gate in gates
        ]
        gate_sums, outs = [], []
        for h in range(CHUNKS):
            earlier = tuple(steps[0] for steps in slabs[:h])
            gate_sums.append(contract_last(after(gates[h], *earlier), gate_weight))
        for h in range(CHUNKS):
            up_all = gather(after(grads[h][1], gate_sums[h]))
            earlier = tuple(steps[min(h + 1 - n, len(steps) - 1)] for n, steps in enumerate(slabs[: h + 2]))
            outs.append(scatter(gate_sums[h] + contract_last(after(up_all, *earlier), up_weight)))
        factor = lax.dot_general(
            jnp.concatenate([steps[-1] for steps in slabs], axis=0),
            jnp.concatenate(gates, axis=0),
            (((0,), (0,)), ((), ())),
            preferred_element_type=jnp.float32,
        )
        input_grad = jnp.concatenate([x.astype(jnp.bfloat16) for x in outs], axis=0)
        return (input_grad, factor / tokens)

    return shards


def solution(mesh):
    return jax.shard_map(
        make_shards(mesh.shape["row"], mesh.shape["col"]),
        mesh=mesh,
        in_specs=(
            P("col", "row"),
            P("row", "col"),
            P("row", "col"),
            P("row", "col"),
            P("row", "col"),
            P("col", "row"),
        ),
        out_specs=(P("col", "row"), P("row", "col")),
        check_vma=False,
    )
```

```python
import jax
import jax.numpy as jnp
from jax import lax
from jax.sharding import PartitionSpec as P

CHUNKS = 2
SLAB_DEV = 896


def contract_last(left, right):
    return lax.dot_general(
        left, right, (((1,), (1,)), ((), ())), preferred_element_type=jnp.float32
    )


def swap(block, axis, size, bit):
    return lax.ppermute(block, axis, [(i, i ^ bit) for i in range(size)])


def bits_down(size):
    bit = size // 2
    while bit:
        yield bit
        bit //= 2


def gather_relative(block, axis, size):
    pieces = {0: block}
    for bit in bits_down(size):
        for k in sorted(pieces):
            pieces[k | bit] = swap(pieces[k], axis, size, bit)
    return [pieces[k] for k in range(size)]


def halving_order(size):
    if size == 1:
        return [0]
    rest = halving_order(size // 2)
    return [2 * k + 1 for k in rest] + [2 * k for k in rest]


def after(value, *earlier):
    return lax.optimization_barrier((value,) + earlier)[0]


def halving(total, axis, size):
    m = total.shape[0] // size
    last = None
    received = []
    bit, left = 1, size
    while left > 1:
        half = left // 2 * m
        sent = total[:half]
        for x in received:
            sent = sent + x[:half].astype(jnp.float32)
        received = [x[half:] for x in received]
        last = sent.astype(jnp.bfloat16)
        received.append(swap(last, axis, size, bit))
        total = total[half:]
        bit, left = bit * 2, left // 2
    for x in received:
        total = total + x.astype(jnp.float32)
    return total, last


def pick(stacked, index, m):
    return lax.dynamic_slice_in_dim(stacked, index * m, m, 0)


def swiglu_grads(hidden_grad, gate_preact, up_preact):
    gate_float = gate_preact.astype(jnp.float32)
    up_float = up_preact.astype(jnp.float32)
    logistic = jax.nn.sigmoid(gate_float)
    derivative = logistic * (1.0 + gate_float * (1.0 - logistic))
    grad_gate = (hidden_grad * up_float * derivative).astype(jnp.bfloat16)
    grad_up = (hidden_grad * gate_float * logistic).astype(jnp.bfloat16)
    return (grad_gate, grad_up)


def make_shards(rows, cols):
    def shards(output_grad, gate_preact, up_preact, gate_weight, up_weight, down_weight):
        units_dev = gate_weight.shape[1]
        part = output_grad.shape[0] // CHUNKS
        tokens = output_grad.shape[0] * cols
        per_row = cols // rows
        row, col = lax.axis_index("row"), lax.axis_index("col")
        offset = (row * SLAB_DEV) % units_dev
        holders = [r * SLAB_DEV // units_dev for r in range(rows)]
        from_holder = col ^ ((row * SLAB_DEV) // units_dev)

        def broadcast(slab):
            steps, unseen = [], cols - 1
            for bit in [1] + [b for b in bits_down(cols) if b > 1]:
                reached = [k for k in range(cols) if not k & unseen]
                pairs = [
                    (r * cols + (holders[r] ^ k), r * cols + (holders[r] ^ k ^ bit))
                    for r in range(rows)
                    for k in reached
                ]
                unseen -= bit
                arrived = lax.ppermute(slab, ("row", "col"), pairs)
                here = ((from_holder & bit) != 0) & ((from_holder & unseen) == 0)
                slab = jnp.where(here, arrived, slab)
                steps.append(slab)
            return steps

        def local_tokens(preact, h):
            split = preact.reshape((per_row, CHUNKS, part, preact.shape[1]))
            return split[:, h].reshape((per_row * part, preact.shape[1]))

        def cotangent(h):
            pieces = gather_relative(output_grad[h * part : (h + 1) * part], "col", cols)
            stacked = jnp.concatenate(pieces, axis=0)
            wanted = [
                col ^ ((row ^ j) * per_row + sub)
                for j in halving_order(rows)
                for sub in range(per_row)
            ]
            return jnp.concatenate([pick(stacked, k, part) for k in wanted], axis=0)

        def scatter(total):
            blocks = []
            for k in halving_order(cols):
                target = col ^ k
                position = (row ^ (target // per_row)) * per_row + target % per_row
                blocks.append(pick(total, position, part))
            return halving(jnp.concatenate(blocks, axis=0), "col", cols)[0]

        def gather(block):
            return jnp.concatenate(gather_relative(block, "row", rows), axis=0)

        grads, earlier = [], ()
        for h in range(CHUNKS):
            part_sum = contract_last(after(cotangent(h), *earlier), down_weight)
            hidden_grad, last = halving(part_sum, "row", rows)
            earlier = (last,)
            grads.append(
                swiglu_grads(hidden_grad, local_tokens(gate_preact, h), local_tokens(up_preact, h))
            )
        gates = [gather(grad_gate) for grad_gate, _ in grads]
        slabs = [
            broadcast(lax.dynamic_slice_in_dim(gate, offset, SLAB_DEV, 1)) for gate in gates
        ]
        gate_sums, outs = [], []
        for h in range(CHUNKS):
            gate_sums.append(contract_last(gates[h], gate_weight))
        for h in range(CHUNKS):
            up_all = gather(after(grads[h][1], gate_sums[h]))
            earlier = [slabs[n][h - n] for n in range(h + 1)]
            outs.append(scatter(gate_sums[h] + contract_last(after(up_all, *earlier), up_weight)))
        factor = lax.dot_general(
            jnp.concatenate([steps[-1] for steps in slabs], axis=0),
            jnp.concatenate(gates, axis=0),
            (((0,), (0,)), ((), ())),
            preferred_element_type=jnp.float32,
        )
        input_grad = jnp.concatenate([x.astype(jnp.bfloat16) for x in outs], axis=0)
        return (input_grad, factor / tokens)

    return shards


def solution(mesh):
    return jax.shard_map(
        make_shards(mesh.shape["row"], mesh.shape["col"]),
        mesh=mesh,
        in_specs=(
            P("col", "row"),
            P("row", "col"),
            P("row", "col"),
            P("row", "col"),
            P("row", "col"),
            P("col", "row"),
        ),
        out_specs=(P("col", "row"), P("row", "col")),
        check_vma=False,
    )
```
